128 devices in a mesh: src: 16 (over z, y_lo, core), tgt: 8 (over x, y_hi).
Axes of the slice: x: 4, y: 4 (y_hi: 2, y_lo: 2; y = y_hi * 2 + y_lo), z: 4, core: 2. Of those that a mesh axis runs over, the one named last changes fastest.
Arguments:
- charges: bfloat16 [2097152, 128], P(('src', 'tgt')), may hold values from -6 to 6
- project: bfloat16 [2048, 128, 1024], P(('src', 'tgt')), may hold values from -0.1875 to 0.1875
- own_transfer: bfloat16 [4, 2048, 64, 128], P(None, ('src', 'tgt')), may hold values from -0.375 to 0.375
- cross_transfer: bfloat16 [4, 2048, 64, 128], P(None, ('src', 'tgt')), may hold values from -0.375 to 0.375
- evaluate: bfloat16 [2048, 1024, 128], P(('src', 'tgt')), may hold values from -0.5 to 0.5
Outputs:
- potential: bfloat16 [2, 2097152, 128], P(None, ('src', 'tgt'))
The draws below stay inside these ranges and needn't reach their ends.
All inputs are finite; a program needn't handle non-finite values.
Results may differ from the reference program's by a relative error of at most 0.009.
Values may be sent and summed in bfloat16 or wider, within the bound.
No kernel may reach another device: no remote copies, remote signals or barrier semaphores. Data moves between devices by JAX's collectives and lax.ppermute only.
A program may use at most 128 MiB of HBM per device.

```python
import jax
import jax.numpy as jnp
from jax import lax

RANK = 64
P_SIZE = 1024
R = 128
LEVELS = 4
M = 16
NB = 2048
N_SRC = 16
N_TGT = 8


def level_of(own_key, extent, split, low, top_value):
    def one(axis_at, shards_of):
        heights = jax.random.uniform(jax.random.fold_in(jax.random.fold_in(own_key, 6), axis_at), (shards_of,), jnp.float32, low / len(split), top_value / len(split))
        return jnp.repeat(jnp.exp(heights), extent[axis_at] // shards_of).reshape((-1,) + (1,) * (len(extent) - axis_at - 1))

    factor_of = one(*split[0])
    for cut in split[1:]:
        factor_of = factor_of * one(*cut)
    return factor_of


def gaussian(key, shape, deviation, bound, cuts=(), held_as=jnp.bfloat16):
    drawn = deviation * jax.random.normal(key, shape, jnp.float32)
    if cuts:
        drawn = drawn * level_of(key, shape, cuts, -0.22, 0.18)
    return jnp.clip(drawn, -bound, bound).astype(held_as)


def setup_inputs(seed: int = 0) -> dict:
    splits = jax.random.split(jax.random.key(seed), 6)
    charges = gaussian(splits[0], (NB * P_SIZE, R), 1.0, 6.0, ((0, 128),))
    project = gaussian(splits[1], (NB, 2 * RANK, P_SIZE), P_SIZE ** -0.5, 0.1875, ((0, 128),))
    own_transfer = gaussian(splits[2], (LEVELS, NB, RANK, 2 * RANK), (4 * RANK) ** -0.5, 0.375, ((1, 128),))
    cross_transfer = gaussian(splits[3], (LEVELS, NB, RANK, 2 * RANK), (4 * RANK) ** -0.5, 0.375, ((1, 128),))
    evaluate = gaussian(splits[4], (NB, P_SIZE, 2 * RANK), (2 * RANK) ** -0.5, 0.5, ((0, 128),))
    return dict(charges=charges, project=project, own_transfer=own_transfer, cross_transfer=cross_transfer, evaluate=evaluate)


def rotate_pair(coeffs):
    half_rank = coeffs.shape[1] // 2
    real_rows = coeffs[:, :half_rank]
    imag_rows = coeffs[:, half_rank:]
    flipped = jnp.concatenate([real_rows, -imag_rows], axis=1)
    swapped = jnp.concatenate([imag_rows, real_rows], axis=1)
    return flipped, swapped


def complex_apply(matrices, coeffs):
    flipped, swapped = rotate_pair(coeffs)
    widened = matrices.astype(jnp.float32)
    real_part = jnp.einsum("bkj,bjr->bkr", widened, flipped.astype(jnp.float32))
    imag_part = jnp.einsum("bkj,bjr->bkr", widened, swapped.astype(jnp.float32))
    return jnp.concatenate([real_part, imag_part], axis=1)


def leaf_group(operands):
    charge_block, project_block = operands
    summed = jnp.einsum("bkp,bpr->bkr", project_block.astype(jnp.float32), charge_block.astype(jnp.float32))
    return summed.astype(jnp.bfloat16)


def far_group(operands):
    switched_block, evaluate_block = operands
    flipped, swapped = rotate_pair(switched_block)
    widened = evaluate_block.astype(jnp.float32)
    real_part = jnp.einsum("bpj,bjr->bpr", widened, flipped.astype(jnp.float32))
    imag_part = jnp.einsum("bpj,bjr->bpr", widened, swapped.astype(jnp.float32))
    return jnp.stack([real_part, imag_part]).astype(jnp.bfloat16)


def reference(charges, project, own_transfer, cross_transfer, evaluate):
    group_count = N_SRC * N_TGT
    charge_groups = charges.reshape(group_count, M, P_SIZE, R)
    project_groups = project.reshape(group_count, M, 2 * RANK, P_SIZE)
    coeffs = lax.map(leaf_group, (charge_groups, project_groups)).reshape(NB, 2 * RANK, R)
    bit_count = N_SRC.bit_length() - 1
    for height in range(LEVELS):
        spacing = 2 ** (height % bit_count)
        arranged = coeffs.reshape(N_SRC // (2 * spacing), 2, spacing, N_TGT * M, 2 * RANK, R)
        partner = arranged[:, ::-1].reshape(NB, 2 * RANK, R)
        summed = complex_apply(own_transfer[height], coeffs) + complex_apply(cross_transfer[height], partner)
        coeffs = summed.astype(jnp.bfloat16)
    per_group = M // N_TGT
    switched = coeffs.reshape(N_SRC, N_TGT, N_TGT, per_group, 2 * RANK, R)
    switched = switched.transpose(0, 2, 1, 3, 4, 5).reshape(group_count, M, 2 * RANK, R)
    evaluate_groups = evaluate.reshape(group_count, M, P_SIZE, 2 * RANK)
    evaluated = lax.map(far_group, (switched, evaluate_groups))
    return evaluated.transpose(1, 0, 2, 3, 4).reshape(2, NB * P_SIZE, R)
```

```python
import jax
import jax.numpy as jnp
from jax import lax
from jax.experimental import pallas as pl
from jax.experimental.pallas import tpu as pltpu
from jax.sharding import PartitionSpec as P

F32 = jnp.float32
BF16 = jnp.bfloat16
RANK2 = 128
POINTS = 1024
COLS = 128
MIB = 1024 * 1024
VMEM = pl.BlockSpec(memory_space=pltpu.VMEM)
ANY = pl.BlockSpec(memory_space=pl.ANY)


def pairs_by(mask, size):
    return [(i, i ^ mask) for i in range(size)]


def pair_at(j, b):
    tgt = lax.axis_index("tgt")
    return tgt ^ (j * 2 + b)


def rotated(c):
    half = c.shape[0] // 2
    re, im = c[:half], c[half:]
    return jnp.concatenate([jnp.concatenate([re, -im], axis=0), jnp.concatenate([im, re], axis=0)], axis=1)


def butterfly(own, cross, own_rotated, partner_rotated):
    matrices = jnp.concatenate([own, cross], axis=1)
    operand = jnp.concatenate([own_rotated, partner_rotated], axis=0)
    both = jnp.dot(matrices, operand, preferred_element_type=F32)
    cols = both.shape[1] // 2
    return jnp.concatenate([both[:, :cols], both[:, cols:]], axis=0).astype(BF16)


def leaf(project, charges, chunk):
    def kernel(project, charges, out, rows, points, row_sems, point_sems):
        loads = []
        for j in range(4):
            pair = pair_at(j, chunk)
            row_load = pltpu.make_async_copy(project.at[pl.ds(pair * 2, 2)], rows.at[pl.ds(j * 2, 2)], row_sems.at[j])
            point_load = pltpu.make_async_copy(charges.at[pl.ds(pair * 2 * POINTS, 2 * POINTS)], points.at[j], point_sems.at[j])
            row_load.start()
            point_load.start()
            loads.append((row_load, point_load))
        for j, (row_load, point_load) in enumerate(loads):
            row_load.wait()
            point_load.wait()
            for v in range(2):
                block = points[j, v * POINTS : (v + 1) * POINTS, :]
                out[j, v] = jnp.dot(rows[j * 2 + v], block, preferred_element_type=F32).astype(BF16)

    return pl.pallas_call(
        kernel,
        in_specs=[ANY, ANY],
        out_specs=VMEM,
        out_shape=jax.ShapeDtypeStruct((4, 2, RANK2, COLS), BF16),
        scratch_shapes=[
            pltpu.VMEM((8, RANK2, POINTS), BF16),
            pltpu.VMEM((4, 2 * POINTS, COLS), BF16),
            pltpu.SemaphoreType.DMA((4,)),
            pltpu.SemaphoreType.DMA((4,)),
        ],
        compiler_params=pltpu.CompilerParams(vmem_limit_bytes=58 * MIB),
        cost_estimate=pl.CostEstimate(flops=8 * 2 * 128 * 128 * 1024, bytes_accessed=4 * MIB, transcendentals=0),
        name="leaf",
    )(project, charges)


def level(own, cross, coeffs, partner, height, chunk, split):
    def kernel(own, cross, coeffs, partner, *outs):
        for j in range(4):
            pair = pair_at(j, chunk)
            for v in range(2):
                m = pair * 2 + v
                new = butterfly(own[height, m], cross[height, m], rotated(coeffs[j, v]), rotated(partner[j, v]))
                if split:
                    outs[j][v] = new
                else:
                    outs[0][j, v] = new

    one = jax.ShapeDtypeStruct((2, RANK2, COLS), BF16)
    return pl.pallas_call(
        kernel,
        in_specs=[VMEM] * 4,
        out_specs=[VMEM] * 4 if split else VMEM,
        out_shape=[one] * 4 if split else jax.ShapeDtypeStruct((4, 2, RANK2, COLS), BF16),
        compiler_params=pltpu.CompilerParams(vmem_limit_bytes=8 * MIB),
        cost_estimate=pl.CostEstimate(flops=8 * 2 * 64 * 256 * 256, bytes_accessed=MIB, transcendentals=0),
        name="level",
    )(own, cross, coeffs, partner)


def far_field(pieces, evaluate, chunk, so_far=None):
    def kernel(c0, c1, c2, c3, matrices, *rest):
        out, results, sems = rest[-3:]
        copies = []
        for j, piece in enumerate((c0, c1, c2, c3)):
            pair = pair_at(j, chunk)
            for v in range(2):
                n, block = j * 2 + v, pair * 2 + v
                turned = rotated(piece[v])
                for part in range(4):
                    span = pl.ds(part * (POINTS // 4), POINTS // 4)
                    both = jnp.dot(matrices[block, span, :], turned, preferred_element_type=F32)
                    results[n, 0, span, :] = both[:, :COLS].astype(BF16)
                    results[n, 1, span, :] = both[:, COLS:].astype(BF16)
                for c in range(2):
                    copy = pltpu.make_async_copy(results.at[n, c], out.at[c, pl.ds(block * POINTS, POINTS)], sems.at[n * 2 + c])
                    copy.start()
                    copies.append(copy)
        for copy in copies:
            copy.wait()

    operands = [*pieces, evaluate] + ([] if so_far is None else [so_far])
    return pl.pallas_call(
        kernel,
        in_specs=[VMEM] * 5 + ([] if so_far is None else [ANY]),
        out_specs=ANY,
        out_shape=jax.ShapeDtypeStruct((2, 16 * POINTS, COLS), BF16),
        scratch_shapes=[pltpu.VMEM((8, 2, POINTS, COLS), BF16), pltpu.SemaphoreType.DMA((16,))],
        input_output_aliases={} if so_far is None else {5: 0},
        compiler_params=pltpu.CompilerParams(vmem_limit_bytes=16 * MIB),
        cost_estimate=pl.CostEstimate(flops=8 * 2 * 1024 * 128 * 256, bytes_accessed=6 * MIB, transcendentals=0),
        name="far_field",
    )(*operands)


def shards(charges, project, own_transfer, cross_transfer, evaluate):
    def levels(chunk):
        coeffs = leaf(project, charges, chunk)
        for height in range(4):
            partner = lax.ppermute(coeffs, "src", pairs_by(1 << height, 16))
            coeffs = level(own_transfer, cross_transfer, coeffs, partner, height, chunk, split=height == 3 and chunk == 0)
        if chunk:
            coeffs = lax.ppermute(coeffs, "tgt", pairs_by(1, 8))
            coeffs = [coeffs[j] for j in range(4)]
        return [lax.ppermute(coeffs[j], "tgt", pairs_by(2 * j, 8)) if j else coeffs[j] for j in range(4)]

    crossed = levels(1)
    straight = levels(0)
    potential = far_field(crossed, evaluate, 1)
    return far_field(straight, evaluate, 0, potential)


def solution(mesh):
    in_specs = (
        P(("src", "tgt"), None),
        P(("src", "tgt"), None, None),
        P(None, ("src", "tgt"), None, None),
        P(None, ("src", "tgt"), None, None),
        P(("src", "tgt"), None, None),
    )
    out_specs = P(None, ("src", "tgt"), None)
    return jax.shard_map(shards, mesh=mesh, in_specs=in_specs, out_specs=out_specs, check_vma=False)
```

```python
import jax
import jax.numpy as jnp
from jax import lax
from jax.experimental import pallas as pl
from jax.experimental.pallas import tpu as pltpu
from jax.sharding import PartitionSpec as P

F32 = jnp.float32
BF16 = jnp.bfloat16
RANK2 = 128
POINTS = 1024
COLS = 128
MIB = 1024 * 1024
VMEM = pl.BlockSpec(memory_space=pltpu.VMEM)
ANY = pl.BlockSpec(memory_space=pl.ANY)

CHUNKS = {"A": ((0, 1), (1, 1), (2, 1), (3, 1)), "B": ((0, 0), (1, 0), (2, 0), (3, 0))}


def pairs_by(mask, size):
    return [(i, i ^ mask) for i in range(size)]


def place_of(pair):
    return lax.axis_index("tgt") ^ (pair[0] * 2 + pair[1])


def rotated(c):
    half = c.shape[0] // 2
    re, im = c[:half], c[half:]
    return jnp.concatenate([jnp.concatenate([re, -im], axis=0), jnp.concatenate([im, re], axis=0)], axis=1)


def butterfly(own, cross, own_rotated, partner_rotated):
    matrices = jnp.concatenate([own, cross], axis=1)
    operand = jnp.concatenate([own_rotated, partner_rotated], axis=0)
    both = jnp.dot(matrices, operand, preferred_element_type=F32)
    cols = both.shape[1] // 2
    return jnp.concatenate([both[:, :cols], both[:, cols:]], axis=0).astype(BF16)


def coeffs_shape(pairs):
    return jax.ShapeDtypeStruct((len(pairs), 2, RANK2, COLS), BF16)


def leaf(after, project, charges, pairs):
    count = len(pairs)

    def kernel(project, charges, *rest):
        out, rows, points, row_sems, point_sems = rest[-5:]
        loads = []
        for n, pair in enumerate(pairs):
            place = place_of(pair)
            row_load = pltpu.make_async_copy(project.at[pl.ds(place * 2, 2)], rows.at[pl.ds(n * 2, 2)], row_sems.at[n])
            point_load = pltpu.make_async_copy(charges.at[pl.ds(place * 2 * POINTS, 2 * POINTS)], points.at[n], point_sems.at[n])
            row_load.start()
            point_load.start()
            loads.append((row_load, point_load))
        for n, (row_load, point_load) in enumerate(loads):
            row_load.wait()
            point_load.wait()
            for v in range(2):
                block = points[n, v * POINTS : (v + 1) * POINTS, :]
                out[n, v] = jnp.dot(rows[n * 2 + v], block, preferred_element_type=F32).astype(BF16)

    return pl.pallas_call(
        kernel,
        in_specs=[ANY] * (2 + len(after)),
        out_specs=VMEM,
        out_shape=coeffs_shape(pairs),
        scratch_shapes=[
            pltpu.VMEM((count * 2, RANK2, POINTS), BF16),
            pltpu.VMEM((count, 2 * POINTS, COLS), BF16),
            pltpu.SemaphoreType.DMA((count,)),
            pltpu.SemaphoreType.DMA((count,)),
        ],
        compiler_params=pltpu.CompilerParams(vmem_limit_bytes=50 * MIB),
        cost_estimate=pl.CostEstimate(flops=count * 4 * 128 * 128 * 1024, bytes_accessed=count * MIB, transcendentals=0),
        name="leaf",
    )(project, charges, *after)


def level(after, own, cross, coeffs, partner, height, pairs):
    def kernel(own, cross, coeffs, partner, *rest):
        out = rest[-1]
        for n, pair in enumerate(pairs):
            place = place_of(pair)
            for v in range(2):
                m = place * 2 + v
                out[n, v] = butterfly(own[height, m], cross[height, m], rotated(coeffs[n, v]), rotated(partner[n, v]))

    return pl.pallas_call(
        kernel,
        in_specs=[VMEM] * 4 + [ANY] * len(after),
        out_specs=VMEM,
        out_shape=coeffs_shape(pairs),
        compiler_params=pltpu.CompilerParams(vmem_limit_bytes=8 * MIB),
        cost_estimate=pl.CostEstimate(flops=len(pairs) * 4 * 64 * 256 * 256, bytes_accessed=MIB // 2, transcendentals=0),
        name="level",
    )(own, cross, coeffs, partner, *after)


def far_field(so_far, pieces, evaluate):
    count = len(pieces)

    def kernel(*refs):
        arrays, matrices = refs[:count], refs[count]
        out, results, sems = refs[-3:]
        copies = []
        for j, (pair, piece) in enumerate(zip(pieces, arrays)):
            place = place_of(pair)
            for v in range(2):
                n, block = j * 2 + v, place * 2 + v
                turned = rotated(piece[0, v])
                for part in range(4):
                    span = pl.ds(part * (POINTS // 4), POINTS // 4)
                    both = jnp.dot(matrices[block, span, :], turned, preferred_element_type=F32)
                    results[n, 0, span, :] = both[:, :COLS].astype(BF16)
                    results[n, 1, span, :] = both[:, COLS:].astype(BF16)
                for c in range(2):
                    copy = pltpu.make_async_copy(results.at[n, c], out.at[c, pl.ds(block * POINTS, POINTS)], sems.at[n * 2 + c])
                    copy.start()
                    copies.append(copy)
        for copy in copies:
            copy.wait()

    shape = jax.ShapeDtypeStruct((2, 16 * POINTS, COLS), BF16)
    first = so_far.shape != shape.shape
    return pl.pallas_call(
        kernel,
        in_specs=[VMEM] * (count + 1) + [ANY],
        out_specs=ANY,
        out_shape=shape,
        scratch_shapes=[pltpu.VMEM((count * 2, 2, POINTS, COLS), BF16), pltpu.SemaphoreType.DMA((count * 4,))],
        input_output_aliases={} if first else {count + 1: 0},
        compiler_params=pltpu.CompilerParams(vmem_limit_bytes=16 * MIB),
        cost_estimate=pl.CostEstimate(flops=count * 4 * 1024 * 128 * 256, bytes_accessed=count * MIB * 3 // 2, transcendentals=0),
        name="far_field",
    )(*pieces.values(), evaluate, so_far)


def shards(charges, project, own_transfer, cross_transfer, evaluate):
    now, partner, pieces = {}, {}, {}
    after = []

    def proceed(name, new, height):
        after[:] = [new]
        now[name] = new
        if height < 4:
            partner[name] = lax.ppermute(new, "src", pairs_by(1 << height, 16))
        elif CHUNKS[name][0][1]:
            now[name] = lax.ppermute(new, "tgt", pairs_by(1, 8))
        if height == 4:
            for n, (j, b) in enumerate(CHUNKS[name]):
                piece = now[name][n : n + 1]
                pieces[j, b] = lax.ppermute(piece, "tgt", pairs_by(2 * j, 8)) if j else piece

    potential = own_transfer
    for name, stage in ORDER:
        if stage == "leaf":
            proceed(name, leaf(after, project, charges, CHUNKS[name]), 0)
        elif stage == "far":
            potential = far_field(potential, {pair: pieces[pair] for pair in name}, evaluate)
        else:
            new = level(after, own_transfer, cross_transfer, now[name], partner[name], stage, CHUNKS[name])
            proceed(name, new, stage + 1)
    return potential


ORDER = (
    ("A", "leaf"), ("A", 0), ("B", "leaf"), ("A", 1), ("B", 0), ("A", 2), ("B", 1), ("A", 3), ("B", 2), ("B", 3),
    (((0, 1), (1, 1), (2, 1), (3, 1), (0, 0)), "far"), (((1, 0), (3, 0)), "far"), (((2, 0),), "far"),
)


def solution(mesh):
    in_specs = (
        P(("src", "tgt"), None),
        P(("src", "tgt"), None, None),
        P(None, ("src", "tgt"), None, None),
        P(None, ("src", "tgt"), None, None),
        P(("src", "tgt"), None, None),
    )
    out_specs = P(None, ("src", "tgt"), None)
    return jax.shard_map(shards, mesh=mesh, in_specs=in_specs, out_specs=out_specs, check_vma=False)
```

```python
import jax
import jax.numpy as jnp
from jax import lax
from jax.experimental import pallas as pl
from jax.experimental.pallas import tpu as pltpu
from jax.sharding import PartitionSpec as P

F32 = jnp.float32
BF16 = jnp.bfloat16
RANK2 = 128
POINTS = 1024
COLS = 128
MIB = 1024 * 1024
VMEM = pl.BlockSpec(memory_space=pltpu.VMEM)
ANY = pl.BlockSpec(memory_space=pl.ANY)

CHUNKS = {"A": ((0, 1), (1, 1)), "B": ((2, 1), (3, 1)), "C": ((0, 0), (1, 0), (2, 0), (3, 0))}


def pairs_by(mask, size):
    return [(i, i ^ mask) for i in range(size)]


def place_of(pair):
    return lax.axis_index("tgt") ^ (pair[0] * 2 + pair[1])


def rotated(c):
    half = c.shape[0] // 2
    re, im = c[:half], c[half:]
    return jnp.concatenate([jnp.concatenate([re, -im], axis=0), jnp.concatenate([im, re], axis=0)], axis=1)


def butterfly(own, cross, own_rotated, partner_rotated):
    matrices = jnp.concatenate([own, cross], axis=1)
    operand = jnp.concatenate([own_rotated, partner_rotated], axis=0)
    both = jnp.dot(matrices, operand, preferred_element_type=F32)
    cols = both.shape[1] // 2
    return jnp.concatenate([both[:, :cols], both[:, cols:]], axis=0).astype(BF16)


def coeffs_shape(pairs):
    return jax.ShapeDtypeStruct((len(pairs), 2, RANK2, COLS), BF16)


def leaf(after, project, charges, pairs, outs):
    count = len(pairs)
    each = count // outs

    def kernel(project, charges, *rest):
        outputs, (rows, points, row_sems, point_sems) = rest[len(after) : -4], rest[-4:]
        loads = []
        for n, pair in enumerate(pairs):
            place = place_of(pair)
            row_load = pltpu.make_async_copy(project.at[pl.ds(place * 2, 2)], rows.at[pl.ds(n * 2, 2)], row_sems.at[n])
            point_load = pltpu.make_async_copy(charges.at[pl.ds(place * 2 * POINTS, 2 * POINTS)], points.at[n], point_sems.at[n])
            row_load.start()
            point_load.start()
            loads.append((row_load, point_load))
        for n, (row_load, point_load) in enumerate(loads):
            row_load.wait()
            point_load.wait()
            for v in range(2):
                block = points[n, v * POINTS : (v + 1) * POINTS, :]
                outputs[n // each][n % each, v] = jnp.dot(rows[n * 2 + v], block, preferred_element_type=F32).astype(BF16)

    return pl.pallas_call(
        kernel,
        in_specs=[ANY] * (2 + len(after)),
        out_specs=[VMEM] * outs,
        out_shape=[coeffs_shape(pairs[:each])] * outs,
        scratch_shapes=[
            pltpu.VMEM((count * 2, RANK2, POINTS), BF16),
            pltpu.VMEM((count, 2 * POINTS, COLS), BF16),
            pltpu.SemaphoreType.DMA((count,)),
            pltpu.SemaphoreType.DMA((count,)),
        ],
        compiler_params=pltpu.CompilerParams(vmem_limit_bytes=50 * MIB),
        cost_estimate=pl.CostEstimate(flops=count * 4 * 128 * 128 * 1024, bytes_accessed=count * MIB, transcendentals=0),
        name="leaf",
    )(project, charges, *after)


def level(after, own, cross, coeffs, partners, height, pairs, outs):
    parts = len(coeffs)
    each, out_each = len(pairs) // parts, len(pairs) // outs

    def kernel(own, cross, *rest):
        coeffs, partners, outputs = rest[:parts], rest[parts : 2 * parts], rest[2 * parts + len(after) :]
        for n, pair in enumerate(pairs):
            place = place_of(pair)
            for v in range(2):
                m = place * 2 + v
                mine, theirs = coeffs[n // each][n % each, v], partners[n // each][n % each, v]
                new = butterfly(own[height, m], cross[height, m], rotated(mine), rotated(theirs))
                outputs[n // out_each][n % out_each, v] = new

    return pl.pallas_call(
        kernel,
        in_specs=[VMEM] * (2 + 2 * parts) + [ANY] * len(after),
        out_specs=[VMEM] * outs,
        out_shape=[coeffs_shape(pairs[:out_each])] * outs,
        compiler_params=pltpu.CompilerParams(vmem_limit_bytes=8 * MIB),
        cost_estimate=pl.CostEstimate(flops=len(pairs) * 4 * 64 * 256 * 256, bytes_accessed=MIB // 2, transcendentals=0),
        name="level",
    )(own, cross, *coeffs, *partners, *after)


def far_field(so_far, pieces, evaluate):
    count = len(pieces)

    def kernel(*refs):
        arrays, matrices = refs[:count], refs[count]
        out, results, sems = refs[-3:]
        copies = []
        for j, (pair, piece) in enumerate(zip(pieces, arrays)):
            place = place_of(pair)
            for v in range(2):
                n, block = j * 2 + v, place * 2 + v
                turned = rotated(piece[0, v])
                for part in range(4):
                    span = pl.ds(part * (POINTS // 4), POINTS // 4)
                    both = jnp.dot(matrices[block, span, :], turned, preferred_element_type=F32)
                    results[n, 0, span, :] = both[:, :COLS].astype(BF16)
                    results[n, 1, span, :] = both[:, COLS:].astype(BF16)
                for c in range(2):
                    copy = pltpu.make_async_copy(results.at[n, c], out.at[c, pl.ds(block * POINTS, POINTS)], sems.at[n * 2 + c])
                    copy.start()
                    copies.append(copy)
        for copy in copies:
            copy.wait()

    shape = jax.ShapeDtypeStruct((2, 16 * POINTS, COLS), BF16)
    first = so_far.shape != shape.shape
    return pl.pallas_call(
        kernel,
        in_specs=[VMEM] * (count + 1) + [ANY],
        out_specs=ANY,
        out_shape=shape,
        scratch_shapes=[pltpu.VMEM((count * 2, 2, POINTS, COLS), BF16), pltpu.SemaphoreType.DMA((count * 4,))],
        input_output_aliases={} if first else {count + 1: 0},
        compiler_params=pltpu.CompilerParams(vmem_limit_bytes=16 * MIB),
        cost_estimate=pl.CostEstimate(flops=count * 4 * 1024 * 128 * 256, bytes_accessed=count * MIB * 3 // 2, transcendentals=0),
        name="far_field",
    )(*pieces.values(), evaluate, so_far)


def shards(charges, project, own_transfer, cross_transfer, evaluate):
    now, partner, pieces = {}, {}, {}
    after = []

    def proceed(name, height, new):
        after[:] = new[:1]
        now[name] = new
        partner[name] = [lax.ppermute(part, "src", pairs_by(1 << height, 16)) for part in new]

    for name, stage, outs in ORDER:
        if stage == "leaf":
            proceed(name, 0, leaf(after, project, charges, CHUNKS[name], outs))
        elif stage < 3:
            new = level(after, own_transfer, cross_transfer, now[name], partner[name], stage, CHUNKS[name], outs)
            proceed(name, stage + 1, new)
        else:
            (new,) = level(after, own_transfer, cross_transfer, now[name], partner[name], stage, CHUNKS[name], 1)
            after[:] = [new]
            if CHUNKS[name][0][1]:
                new = lax.ppermute(new, "tgt", pairs_by(1, 8))
            for n, (j, b) in enumerate(CHUNKS[name]):
                piece = new[n : n + 1]
                pieces[j, b] = lax.ppermute(piece, "tgt", pairs_by(2 * j, 8)) if j else piece
    potential = own_transfer
    for group in FAR:
        potential = far_field(potential, {pair: pieces[pair] for pair in group}, evaluate)
    return potential


ORDER = (
    ("A", "leaf", 1), ("B", "leaf", 1), ("A", 0, 1), ("B", 0, 1), ("C", "leaf", 2), ("A", 1, 1), ("B", 1, 1), ("C", 0, 2), ("A", 2, 1), ("B", 2, 1), ("C", 1, 2), ("A", 3, 1), ("B", 3, 1), ("C", 2, 1), ("C", 3, 1),
)
FAR = (((0, 1), (1, 1), (2, 1), (3, 1), (0, 0)), ((1, 0), (3, 0)), ((2, 0),))


def solution(mesh):
    in_specs = (
        P(("src", "tgt"), None),
        P(("src", "tgt"), None, None),
        P(None, ("src", "tgt"), None, None),
        P(None, ("src", "tgt"), None, None),
        P(("src", "tgt"), None, None),
    )
    out_specs = P(None, ("src", "tgt"), None)
    return jax.shard_map(shards, mesh=mesh, in_specs=in_specs, out_specs=out_specs, check_vma=False)
```

```python
import jax
import jax.numpy as jnp
from jax import lax
from jax.experimental import pallas as pl
from jax.experimental.pallas import tpu as pltpu
from jax.sharding import PartitionSpec as P

F32 = jnp.float32
BF16 = jnp.bfloat16
RANK2 = 128
POINTS = 1024
COLS = 128
MIB = 1024 * 1024
VMEM = pl.BlockSpec(memory_space=pltpu.VMEM)
ANY = pl.BlockSpec(memory_space=pl.ANY)

CHUNKS = {"A": ((0, 1), (1, 1)), "B": ((2, 1), (3, 1)), "C": ((0, 0), (1, 0), (2, 0), (3, 0))}


def pairs_by(mask, size):
    return [(i, i ^ mask) for i in range(size)]


def place_of(pair):
    return lax.axis_index("tgt") ^ (pair[0] * 2 + pair[1])


def rotated(c):
    half = c.shape[0] // 2
    re, im = c[:half], c[half:]
    return jnp.concatenate([jnp.concatenate([re, -im], axis=0), jnp.concatenate([im, re], axis=0)], axis=1)


def butterfly(own, cross, own_rotated, partner_rotated):
    matrices = jnp.concatenate([own, cross], axis=1)
    operand = jnp.concatenate([own_rotated, partner_rotated], axis=0)
    both = jnp.dot(matrices, operand, preferred_element_type=F32)
    cols = both.shape[1] // 2
    return jnp.concatenate([both[:, :cols], both[:, cols:]], axis=0).astype(BF16)


def coeffs_shape(pairs):
    return jax.ShapeDtypeStruct((len(pairs), 2, RANK2, COLS), BF16)


def leaf(after, project, charges, pairs, outs):
    count = len(pairs)
    each = count // outs

    def kernel(project, charges, *rest):
        outputs, (rows, points, row_sems, point_sems) = rest[len(after) : -4], rest[-4:]
        loads = []
        for n, pair in enumerate(pairs):
            place = place_of(pair)
            row_load = pltpu.make_async_copy(project.at[pl.ds(place * 2, 2)], rows.at[pl.ds(n * 2, 2)], row_sems.at[n])
            point_load = pltpu.make_async_copy(charges.at[pl.ds(place * 2 * POINTS, 2 * POINTS)], points.at[n], point_sems.at[n])
            row_load.start()
            point_load.start()
            loads.append((row_load, point_load))
        for n, (row_load, point_load) in enumerate(loads):
            row_load.wait()
            point_load.wait()
            for v in range(2):
                block = points[n, v * POINTS : (v + 1) * POINTS, :]
                outputs[n // each][n % each, v] = jnp.dot(rows[n * 2 + v], block, preferred_element_type=F32).astype(BF16)

    return pl.pallas_call(
        kernel,
        in_specs=[ANY] * (2 + len(after)),
        out_specs=[VMEM] * outs,
        out_shape=[coeffs_shape(pairs[:each])] * outs,
        scratch_shapes=[
            pltpu.VMEM((count * 2, RANK2, POINTS), BF16),
            pltpu.VMEM((count, 2 * POINTS, COLS), BF16),
            pltpu.SemaphoreType.DMA((count,)),
            pltpu.SemaphoreType.DMA((count,)),
        ],
        compiler_params=pltpu.CompilerParams(vmem_limit_bytes=50 * MIB),
        cost_estimate=pl.CostEstimate(flops=count * 4 * 128 * 128 * 1024, bytes_accessed=count * MIB, transcendentals=0),
        name="leaf",
    )(project, charges, *after)


def level(after, own, cross, coeffs, partners, height, pairs, outs):
    parts = len(coeffs)
    each, out_each = len(pairs) // parts, len(pairs) // outs

    def kernel(own, cross, *rest):
        coeffs, partners, outputs = rest[:parts], rest[parts : 2 * parts], rest[2 * parts + len(after) :]
        for n, pair in enumerate(pairs):
            place = place_of(pair)
            for v in range(2):
                m = place * 2 + v
                mine, theirs = coeffs[n // each][n % each, v], partners[n // each][n % each, v]
                new = butterfly(own[height, m], cross[height, m], rotated(mine), rotated(theirs))
                outputs[n // out_each][n % out_each, v] = new

    return pl.pallas_call(
        kernel,
        in_specs=[VMEM] * (2 + 2 * parts) + [ANY] * len(after),
        out_specs=[VMEM] * outs,
        out_shape=[coeffs_shape(pairs[:out_each])] * outs,
        compiler_params=pltpu.CompilerParams(vmem_limit_bytes=8 * MIB),
        cost_estimate=pl.CostEstimate(flops=len(pairs) * 4 * 64 * 256 * 256, bytes_accessed=MIB // 2, transcendentals=0),
        name="level",
    )(own, cross, *coeffs, *partners, *after)


def far_field(so_far, pieces, evaluate):
    count = len(pieces)

    def kernel(*refs):
        arrays, matrices = refs[:count], refs[count]
        out, results, sems = refs[-3:]
        copies = []
        for j, (pair, piece) in enumerate(zip(pieces, arrays)):
            place = place_of(pair)
            for v in range(2):
                n, block = j * 2 + v, place * 2 + v
                turned = rotated(piece[0, v])
                for part in range(4):
                    span = pl.ds(part * (POINTS // 4), POINTS // 4)
                    both = jnp.dot(matrices[block, span, :], turned, preferred_element_type=F32)
                    results[n, 0, span, :] = both[:, :COLS].astype(BF16)
                    results[n, 1, span, :] = both[:, COLS:].astype(BF16)
                for c in range(2):
                    copy = pltpu.make_async_copy(results.at[n, c], out.at[c, pl.ds(block * POINTS, POINTS)], sems.at[n * 2 + c])
                    copy.start()
                    copies.append(copy)
        for copy in copies:
            copy.wait()

    shape = jax.ShapeDtypeStruct((2, 16 * POINTS, COLS), BF16)
    first = so_far.shape != shape.shape
    return pl.pallas_call(
        kernel,
        in_specs=[VMEM] * (count + 1) + [ANY],
        out_specs=ANY,
        out_shape=shape,
        scratch_shapes=[pltpu.VMEM((count * 2, 2, POINTS, COLS), BF16), pltpu.SemaphoreType.DMA((count * 4,))],
        input_output_aliases={} if first else {count + 1: 0},
        compiler_params=pltpu.CompilerParams(vmem_limit_bytes=16 * MIB),
        cost_estimate=pl.CostEstimate(flops=count * 4 * 1024 * 128 * 256, bytes_accessed=count * MIB * 3 // 2, transcendentals=0),
        name="far_field",
    )(*pieces.values(), evaluate, so_far)


def shards(charges, project, own_transfer, cross_transfer, evaluate):
    now, partner, pieces = {}, {}, {}
    after = []

    def proceed(name, height, new):
        after[:] = new[:1]
        now[name] = new
        partner[name] = [lax.ppermute(part, "src", pairs_by(1 << height, 16)) for part in new]

    for name, stage, outs in ORDER:
        if stage == "leaf":
            proceed(name, 0, leaf(after, project, charges, CHUNKS[name], outs))
        elif stage < 3:
            new = level(after, own_transfer, cross_transfer, now[name], partner[name], stage, CHUNKS[name], outs)
            proceed(name, stage + 1, new)
        else:
            (new,) = level(after, own_transfer, cross_transfer, now[name], partner[name], stage, CHUNKS[name], 1)
            after[:] = [new]
            if CHUNKS[name][0][1]:
                new = lax.ppermute(new, "tgt", pairs_by(1, 8))
            for n, (j, b) in enumerate(CHUNKS[name]):
                piece = new[n : n + 1]
                pieces[j, b] = lax.ppermute(piece, "tgt", pairs_by(2 * j, 8)) if j else piece
    potential = own_transfer
    for group in FAR:
        potential = far_field(potential, {pair: pieces[pair] for pair in group}, evaluate)
    return potential


ORDER = (
    ("A", "leaf", 1), ("B", "leaf", 1), ("A", 0, 1), ("B", 0, 1), ("C", "leaf", 2), ("A", 1, 1), ("B", 1, 1), ("C", 0, 2), ("A", 2, 1), ("B", 2, 1), ("C", 1, 2), ("A", 3, 1), ("B", 3, 1), ("C", 2, 1), ("C", 3, 1),
)
FAR = (((0, 1), (1, 1), (2, 1), (3, 1), (0, 0)), ((1, 0), (2, 0), (3, 0)))


def solution(mesh):
    in_specs = (
        P(("src", "tgt"), None),
        P(("src", "tgt"), None, None),
        P(None, ("src", "tgt"), None, None),
        P(None, ("src", "tgt"), None, None),
        P(("src", "tgt"), None, None),
    )
    out_specs = P(None, ("src", "tgt"), None)
    return jax.shard_map(shards, mesh=mesh, in_specs=in_specs, out_specs=out_specs, check_vma=False)
```

```python
import jax
import jax.numpy as jnp
from jax import lax
from jax.experimental import pallas as pl
from jax.experimental.pallas import tpu as pltpu
from jax.sharding import PartitionSpec as P

F32 = jnp.float32
BF16 = jnp.bfloat16
RANK2 = 128
POINTS = 1024
COLS = 128
MIB = 1024 * 1024
VMEM = pl.BlockSpec(memory_space=pltpu.VMEM)
ANY = pl.BlockSpec(memory_space=pl.ANY)

CHUNKS = {"A": ((0, 1), (1, 1)), "B": ((2, 1), (3, 1)), "C": ((0, 0), (1, 0), (2, 0), (3, 0))}


def pairs_by(mask, size):
    return [(i, i ^ mask) for i in range(size)]


def place_of(pair):
    return lax.axis_index("tgt") ^ (pair[0] * 2 + pair[1])


def rotated(c):
    half = c.shape[0] // 2
    re, im = c[:half], c[half:]
    return jnp.concatenate([jnp.concatenate([re, -im], axis=0), jnp.concatenate([im, re], axis=0)], axis=1)


def butterfly(own, cross, own_rotated, partner_rotated):
    matrices = jnp.concatenate([own, cross], axis=1)
    operand = jnp.concatenate([own_rotated, partner_rotated], axis=0)
    both = jnp.dot(matrices, operand, preferred_element_type=F32)
    cols = both.shape[1] // 2
    return jnp.concatenate([both[:, :cols], both[:, cols:]], axis=0).astype(BF16)


def coeffs_shape(pairs):
    return jax.ShapeDtypeStruct((len(pairs), 2, RANK2, COLS), BF16)


def leaf(after, project, charges, pairs, outs):
    count = len(pairs)
    each = count // outs

    def kernel(project, charges, *rest):
        outputs, (rows, points, row_sems, point_sems) = rest[len(after) : -4], rest[-4:]
        loads = []
        for n, pair in enumerate(pairs):
            place = place_of(pair)
            row_load = pltpu.make_async_copy(project.at[pl.ds(place * 2, 2)], rows.at[pl.ds(n * 2, 2)], row_sems.at[n])
            point_load = pltpu.make_async_copy(charges.at[pl.ds(place * 2 * POINTS, 2 * POINTS)], points.at[n], point_sems.at[n])
            row_load.start()
            point_load.start()
            loads.append((row_load, point_load))
        for n, (row_load, point_load) in enumerate(loads):
            row_load.wait()
            point_load.wait()
            for v in range(2):
                block = points[n, v * POINTS : (v + 1) * POINTS, :]
                outputs[n // each][n % each, v] = jnp.dot(rows[n * 2 + v], block, preferred_element_type=F32).astype(BF16)

    return pl.pallas_call(
        kernel,
        in_specs=[ANY] * (2 + len(after)),
        out_specs=[VMEM] * outs,
        out_shape=[coeffs_shape(pairs[:each])] * outs,
        scratch_shapes=[
            pltpu.VMEM((count * 2, RANK2, POINTS), BF16),
            pltpu.VMEM((count, 2 * POINTS, COLS), BF16),
            pltpu.SemaphoreType.DMA((count,)),
            pltpu.SemaphoreType.DMA((count,)),
        ],
        compiler_params=pltpu.CompilerParams(vmem_limit_bytes=50 * MIB),
        cost_estimate=pl.CostEstimate(flops=count * 4 * 128 * 128 * 1024, bytes_accessed=count * MIB, transcendentals=0),
        name="leaf",
    )(project, charges, *after)


def level(after, own, cross, coeffs, partners, height, pairs, outs):
    parts = len(coeffs)
    each, out_each = len(pairs) // parts, len(pairs) // outs

    def kernel(own, cross, *rest):
        coeffs, partners, outputs = rest[:parts], rest[parts : 2 * parts], rest[2 * parts + len(after) :]
        for n, pair in enumerate(pairs):
            place = place_of(pair)
            for v in range(2):
                m = place * 2 + v
                mine, theirs = coeffs[n // each][n % each, v], partners[n // each][n % each, v]
                new = butterfly(own[height, m], cross[height, m], rotated(mine), rotated(theirs))
                outputs[n // out_each][n % out_each, v] = new

    return pl.pallas_call(
        kernel,
        in_specs=[VMEM] * (2 + 2 * parts) + [ANY] * len(after),
        out_specs=[VMEM] * outs,
        out_shape=[coeffs_shape(pairs[:out_each])] * outs,
        compiler_params=pltpu.CompilerParams(vmem_limit_bytes=8 * MIB),
        cost_estimate=pl.CostEstimate(flops=len(pairs) * 4 * 64 * 256 * 256, bytes_accessed=MIB // 2, transcendentals=0),
        name="level",
    )(own, cross, *coeffs, *partners, *after)


def far_field(so_far, pieces, evaluate):
    count = len(pieces)

    def kernel(*refs):
        arrays, matrices = refs[:count], refs[count]
        out, results, sems = refs[-3:]
        copies = []
        for j, (pair, piece) in enumerate(zip(pieces, arrays)):
            place = place_of(pair)
            for v in range(2):
                n, block = j * 2 + v, place * 2 + v
                turned = rotated(piece[0, v])
                for part in range(4):
                    span = pl.ds(part * (POINTS // 4), POINTS // 4)
                    both = jnp.dot(matrices[block, span, :], turned, preferred_element_type=F32)
                    results[n, 0, span, :] = both[:, :COLS].astype(BF16)
                    results[n, 1, span, :] = both[:, COLS:].astype(BF16)
                for c in range(2):
                    copy = pltpu.make_async_copy(results.at[n, c], out.at[c, pl.ds(block * POINTS, POINTS)], sems.at[n * 2 + c])
                    copy.start()
                    copies.append(copy)
        for copy in copies:
            copy.wait()

    shape = jax.ShapeDtypeStruct((2, 16 * POINTS, COLS), BF16)
    first = so_far.shape != shape.shape
    return pl.pallas_call(
        kernel,
        in_specs=[VMEM] * (count + 1) + [ANY],
        out_specs=ANY,
        out_shape=shape,
        scratch_shapes=[pltpu.VMEM((count * 2, 2, POINTS, COLS), BF16), pltpu.SemaphoreType.DMA((count * 4,))],
        input_output_aliases={} if first else {count + 1: 0},
        compiler_params=pltpu.CompilerParams(vmem_limit_bytes=16 * MIB),
        cost_estimate=pl.CostEstimate(flops=count * 4 * 1024 * 128 * 256, bytes_accessed=count * MIB * 3 // 2, transcendentals=0),
        name="far_field",
    )(*pieces.values(), evaluate, so_far)


def shards(charges, project, own_transfer, cross_transfer, evaluate):
    now, partner, pieces = {}, {}, {}
    after = []

    def proceed(name, height, new):
        after[:] = new[:1]
        now[name] = new
        partner[name] = [lax.ppermute(part, "src", pairs_by(1 << height, 16)) for part in new]

    for name, stage, outs in ORDER:
        if stage == "leaf":
            proceed(name, 0, leaf(after, project, charges, CHUNKS[name], outs))
        elif stage < 3:
            new = level(after, own_transfer, cross_transfer, now[name], partner[name], stage, CHUNKS[name], outs)
            proceed(name, stage + 1, new)
        else:
            (new,) = level(after, own_transfer, cross_transfer, now[name], partner[name], stage, CHUNKS[name], 1)
            after[:] = [new]
            if CHUNKS[name][0][1]:
                new = lax.ppermute(new, "tgt", pairs_by(1, 8))
            for n, (j, b) in enumerate(CHUNKS[name]):
                piece = new[n : n + 1]
                pieces[j, b] = lax.ppermute(piece, "tgt", pairs_by(2 * j, 8)) if j else piece
    potential = own_transfer
    for group in FAR:
        potential = far_field(potential, {pair: pieces[pair] for pair in group}, evaluate)
    return potential


ORDER = (
    ("A", "leaf", 1), ("B", "leaf", 1), ("A", 0, 1), ("B", 0, 1), ("C", "leaf", 2), ("A", 1, 1), ("B", 1, 1), ("C", 0, 2), ("A", 2, 1), ("B", 2, 1), ("C", 1, 2), ("A", 3, 1), ("B", 3, 1), ("C", 2, 1), ("C", 3, 1),
)
FAR = (((2, 1), (3, 1), (0, 1), (1, 1), (0, 0)), ((1, 0), (2, 0), (3, 0)))


def solution(mesh):
    in_specs = (
        P(("src", "tgt"), None),
        P(("src", "tgt"), None, None),
        P(None, ("src", "tgt"), None, None),
        P(None, ("src", "tgt"), None, None),
        P(("src", "tgt"), None, None),
    )
    out_specs = P(None, ("src", "tgt"), None)
    return jax.shard_map(shards, mesh=mesh, in_specs=in_specs, out_specs=out_specs, check_vma=False)
```
